768 devices in a mesh: dp: 48 (over y_lo, z), ctx: 16 (over x, y_hi, core).
Axes of the slice: x: 4, y: 8 (y_hi: 2, y_lo: 4; y = y_hi * 4 + y_lo), z: 12, core: 2. Of those that a mesh axis runs over, the one named last changes fastest.
Arguments:
- q_gate: bfloat16 [48, 2048, 2048], P('dp', None, 'ctx'), may hold values from -6 to 6
- k_gate: bfloat16 [48, 2048, 2048], P('dp', None, 'ctx'), may hold values from -6 to 6
- values: bfloat16 [48, 2048, 2048], P('dp', None, 'ctx'), may hold values from -6 to 6
- out_grad: bfloat16 [48, 2048, 2048], P('dp', None, 'ctx'), may hold values from -6 to 6
- decay: float32 [2048], replicated, may hold values from 0.3 to 3
Outputs:
- kernel_grad: float32 [2048, 2048], P(None, 'ctx')
The draws below stay inside these ranges and needn't reach their ends.
All inputs are finite; a program needn't handle non-finite values.
Results may differ from the reference program's by a relative error of at most 0.0041.
Values may be sent and summed in bfloat16 or wider, within the bound.
No kernel may reach another device: no remote copies, remote signals or barrier semaphores. Data moves between devices by JAX's collectives and lax.ppermute only.
A program may use at most 32 MiB of HBM per device.

```python
import math
import jax
import jax.numpy as jnp
from jax import lax

CH = 2048
LD = 128
LENGTH = 2048
BATCH = 48
N_DP = 48
N_CTX = 16


def block_scale(rng, extent, shards, low, high):
    def one(dim, blocks):
        steps = jax.random.uniform(jax.random.fold_in(jax.random.fold_in(rng, 6), dim), (blocks,), jnp.float32, low / len(shards), high / len(shards))
        return jnp.repeat(jnp.exp(steps), extent[dim] // blocks).reshape((-1,) + (1,) * (len(extent) - dim - 1))

    loudness = one(*shards[0])
    for cut in shards[1:]:
        loudness = loudness * one(*cut)
    return loudness


def gaussian(rng, dims, deviation, most, pieces=(), dtype=jnp.bfloat16):
    array = deviation * jax.random.normal(rng, dims, jnp.float32)
    if pieces:
        array = array * block_scale(rng, dims, pieces, -0.22, 0.18)
    return jnp.clip(array, -most, most).astype(dtype)


def setup_inputs(seed: int = 0) -> dict:
    key_list = jax.random.split(jax.random.key(seed), 6)
    return {
        "q_gate": gaussian(key_list[0], (BATCH, CH, LENGTH), 1.0, 6.0, ((0, 48), (2, 16))),
        "k_gate": gaussian(key_list[1], (BATCH, CH, LENGTH), 1.0, 6.0, ((0, 48), (2, 16))),
        "values": gaussian(key_list[2], (BATCH, CH, LENGTH), 1.0, 6.0, ((0, 48), (2, 16))),
        "out_grad": gaussian(key_list[3], (BATCH, CH, LENGTH), 1.0, 6.0, ((0, 48), (2, 16))),
        "decay": jnp.clip(jnp.exp(jax.random.uniform(key_list[4], (CH,), jnp.float32, math.log(0.3), math.log(3.0))), 0.3, 3.0),
    }


def reference(q_gate, k_gate, values, out_grad, decay):
    seq_len = LD * N_CTX
    gated_in = (k_gate.astype(jnp.float32) * values.astype(jnp.float32)).astype(jnp.bfloat16)
    gated_grad = (q_gate.astype(jnp.float32) * out_grad.astype(jnp.float32)).astype(jnp.bfloat16)
    gated_in = lax.optimization_barrier(gated_in).astype(jnp.float32)
    gated_grad = lax.optimization_barrier(gated_grad).astype(jnp.float32)

    def accumulate(carry, pair):
        spec_in = jnp.fft.rfft(pair[0], n=2 * seq_len, axis=-1)
        spec_grad = jnp.fft.rfft(pair[1], n=2 * seq_len, axis=-1)
        product = jnp.conj(spec_in) * spec_grad
        return ((carry[0] + jnp.real(product), carry[1] + jnp.imag(product)), None)
    zeros = jnp.zeros((gated_in.shape[1], seq_len + 1), jnp.float32)
    (sum_real, sum_imag), unused = lax.scan(accumulate, (zeros, zeros), (gated_in, gated_grad))
    cross = jnp.fft.irfft(sum_real + 1j * sum_imag, n=2 * seq_len, axis=-1)[:, :seq_len]
    lags = jnp.arange(seq_len).astype(jnp.float32)
    window = jnp.exp(-decay[:, None] * lags[None, :] / seq_len)
    return (cross * window / math.sqrt(N_DP * seq_len)).astype(jnp.float32)
```

```python
import functools
import math

import jax
import jax.numpy as jnp
import ml_dtypes
import numpy as np
from jax import lax
from jax.experimental import pallas as pl
from jax.experimental.pallas import tpu as pltpu
from jax.sharding import Mesh, PartitionSpec as P

F32 = jnp.float32
BF16 = jnp.bfloat16

SPAN = 128
BLOCKS = 16
FREQS = BLOCKS + 1
PAD_FREQS = FREQS + 1
ROWS = 16
CHANS = ROWS // 2
OUTER = 2 * BLOCKS
TOTAL = OUTER * SPAN


def split16(table):
    high = table.astype(ml_dtypes.bfloat16)
    low = (table - high.astype(np.float64)).astype(ml_dtypes.bfloat16)
    return np.stack([high, low])


@functools.lru_cache(maxsize=None)
def tables():
    k = np.arange(FREQS)[:, None]
    p = np.arange(BLOCKS)[None, :]
    angle = 2.0 * np.pi * (k * p % OUTER) / OUTER
    outer = np.stack([np.cos(angle), -np.sin(angle)], axis=1)
    spread = np.einsum("kcp,rq->kcrpq", outer, np.eye(ROWS))
    spread = spread.reshape(FREQS * 2 * ROWS, BLOCKS * ROWS)
    b = np.arange(SPAN)
    angle = 2.0 * np.pi * (b[:, None] * b[None, :] % SPAN) / SPAN
    cos, sin = np.cos(angle), np.sin(angle)
    forward = np.block([[cos, -sin], [sin, cos]])
    backward = np.block([[cos, sin], [-sin, cos]])
    angle = 2.0 * np.pi * np.arange(PAD_FREQS)[:, None] * b[None, :] / TOTAL
    twist = np.stack([np.cos(angle), np.sin(angle)], axis=1)
    twist = np.broadcast_to(twist[:, :, None, :], (PAD_FREQS, 2, 8, SPAN))
    return (
        split16(spread),
        split16(forward),
        split16(backward),
        np.ascontiguousarray(twist.astype(np.float32)),
    )


def halves(x):
    high = x.astype(BF16)
    return high, (x - high.astype(F32)).astype(BF16)


def dot(a, b):
    return jnp.dot(a, b, preferred_element_type=F32)


def gate_kernel(k_ref, v_ref, q_ref, g_ref, out_ref):
    chans = k_ref.shape[1]
    first = k_ref[0].astype(F32) * v_ref[0].astype(F32)
    second = q_ref[0].astype(F32) * g_ref[0].astype(F32)
    shape = (chans // CHANS, CHANS, SPAN)
    both = jnp.concatenate([first.reshape(shape), second.reshape(shape)], axis=1)
    out_ref[...] = both.astype(BF16)


def gate(q_gate, k_gate, values, out_grad):
    chans = q_gate.shape[1]
    tile = min(chans, 512)
    spec = pl.BlockSpec((1, tile, SPAN), lambda i: (0, i, 0))
    return pl.pallas_call(
        gate_kernel,
        grid=(chans // tile,),
        in_specs=[spec] * 4,
        out_specs=pl.BlockSpec((tile // CHANS, ROWS, SPAN), lambda i: (i, 0, 0)),
        out_shape=jax.ShapeDtypeStruct((chans // CHANS, ROWS, SPAN), BF16),
        name="gate",
    )(k_gate, values, q_gate, out_grad)


def correlate_kernel(x_ref, outer_ref, fwd_ref, bwd_ref, twist_ref, out_ref, high_ref, low_ref):
    seqs = x_ref.shape[0]
    copies = out_ref.shape[0]
    cos = twist_ref[:, 0]
    sin = twist_ref[:, 1]

    def outer_step(s, carry):
        x = x_ref[s].reshape(BLOCKS * ROWS, SPAN)
        y = dot(outer_ref[0], x) + dot(outer_ref[1], x)
        y = y.reshape(FREQS, 2, 2, CHANS, SPAN)
        real, imag = y[:, 0], y[:, 1]
        c = cos[:FREQS, None]
        d = sin[:FREQS, None]
        turned_real = (real * c + imag * d).reshape(FREQS, ROWS, SPAN)
        turned_imag = (imag * c - real * d).reshape(FREQS, ROWS, SPAN)
        rows = pl.ds(pl.multiple_of(s * ROWS, ROWS), ROWS)
        high, low = halves(turned_real)
        high_ref[:, rows, :SPAN] = high
        low_ref[:, rows, :SPAN] = low
        high, low = halves(turned_imag)
        high_ref[:, rows, SPAN:] = high
        low_ref[:, rows, SPAN:] = low
        return carry

    lax.fori_loop(0, seqs, outer_step, 0, unroll=2 if seqs % 2 == 0 else 1)

    cross = []
    for k in range(FREQS):
        high = high_ref[k]
        spec = dot(high, fwd_ref[0]) + (dot(low_ref[k], fwd_ref[0]) + dot(high, fwd_ref[1]))
        spec = spec.reshape(seqs, 2, CHANS, 2 * SPAN)
        in_real, in_imag = spec[:, 0, :, :SPAN], spec[:, 0, :, SPAN:]
        grad_real, grad_imag = spec[:, 1, :, :SPAN], spec[:, 1, :, SPAN:]
        real = jnp.sum(in_real * grad_real + in_imag * grad_imag, axis=0)
        imag = jnp.sum(in_real * grad_imag - in_imag * grad_real, axis=0)
        cross.append(jnp.concatenate([real, imag], axis=1))
    cross.append(jnp.zeros((CHANS, 2 * SPAN), F32))
    cross = jnp.concatenate(cross, axis=0)

    high, low = halves(cross)
    back = dot(high, bwd_ref[0]) + (dot(low, bwd_ref[0]) + dot(high, bwd_ref[1]))
    back = back.reshape(PAD_FREQS, CHANS, 2 * SPAN)
    real, imag = back[:, :, :SPAN], back[:, :, SPAN:]
    turned_real = real * cos - imag * sin
    turned_imag = real * sin + imag * cos
    for n in range(BLOCKS):
        total = None
        for k in range(FREQS):
            weight = (1.0 if k in (0, BLOCKS) else 2.0) / TOTAL
            angle = 2.0 * math.pi * (k * n % OUTER) / OUTER
            term = turned_real[k] * (weight * math.cos(angle))
            if k * n % BLOCKS:
                term = term - turned_imag[k] * (weight * math.sin(angle))
            total = term if total is None else total + term
        for copy in range(copies):
            out_ref[copy, n] = total


def correlate(x, copies):
    seqs = x.shape[0]
    outer, forward, backward, twist = tables()
    rows = seqs * ROWS
    flops = 2 * seqs * 2 * outer.shape[1] * outer.shape[2] * SPAN + 6 * FREQS * rows * 4 * SPAN * SPAN
    return pl.pallas_call(
        correlate_kernel,
        in_specs=[pl.BlockSpec(memory_space=pltpu.VMEM)] * 5,
        out_specs=pl.BlockSpec(memory_space=pltpu.VMEM),
        out_shape=jax.ShapeDtypeStruct((copies, BLOCKS, CHANS, SPAN), F32),
        scratch_shapes=[
            pltpu.VMEM((FREQS, rows, 2 * SPAN), BF16),
            pltpu.VMEM((FREQS, rows, 2 * SPAN), BF16),
        ],
        compiler_params=pltpu.CompilerParams(vmem_limit_bytes=32 * 1024 * 1024),
        cost_estimate=pl.CostEstimate(flops=flops, bytes_accessed=3_000_000, transcendentals=0),
        name="correlate",
    )(x, outer, forward, backward, twist)


CTX = ("x", "y_hi", "core")
NEAR = ("y_lo", "z_lo")


def to_each(x, axes):
    return lax.all_to_all(x, axes, split_axis=0, concat_axis=0, tiled=True)


def body(length, batch, q_gate, k_gate, values, out_grad, decay):
    near = lax.axis_size(NEAR)
    far = lax.axis_size("z_hi")
    gated = gate(q_gate, k_gate, values, out_grad)
    whole = to_each(gated, NEAR + CTX)
    part = correlate(whole.reshape(near, BLOCKS, ROWS, SPAN), far)

    group = BLOCKS * CHANS
    mine = lax.dynamic_slice_in_dim(decay, lax.axis_index(NEAR) * group, group)
    lags = (lax.axis_index(CTX) * SPAN + jnp.arange(SPAN, dtype=jnp.int32)).astype(F32)
    window = jnp.exp(-mine[:, None] * lags[None, :] / length) / math.sqrt(batch * length)

    sent = part.reshape(far * BLOCKS, CHANS, SPAN)
    lag_parts = to_each(sent, ("z_hi",) + CTX).reshape(far, group, SPAN)
    ours = (jnp.sum(lag_parts, axis=0) * window).astype(BF16)
    everyone = to_each(jnp.broadcast_to(ours[None], (near, group, SPAN)), NEAR)
    return everyone.reshape(near * group, SPAN).astype(F32)


def solution(mesh):
    dp, ctx = mesh.devices.shape
    fine = Mesh(
        mesh.devices.reshape(4, dp // 16, 4, ctx // 4, 2, 2),
        ("y_lo", "z_hi", "z_lo") + CTX,
    )
    seqs = ("y_lo", "z_hi", "z_lo")
    return jax.shard_map(
        functools.partial(body, SPAN * ctx, dp),
        mesh=fine,
        in_specs=(P(seqs, None, CTX),) * 4 + (P(),),
        out_specs=P(None, CTX),
        check_vma=False,
    )
```

```python
import functools
import math

import jax
import jax.numpy as jnp
import ml_dtypes
import numpy as np
from jax import lax
from jax.experimental import pallas as pl
from jax.experimental.pallas import tpu as pltpu
from jax.sharding import Mesh, PartitionSpec as P

F32 = jnp.float32
BF16 = jnp.bfloat16

SPAN = 128
BLOCKS = 16
FREQS = BLOCKS + 1
PAD_FREQS = FREQS + 1
ROWS = 16
CHANS = ROWS // 2
OUTER = 2 * BLOCKS
TOTAL = OUTER * SPAN


def split16(table):
    high = table.astype(ml_dtypes.bfloat16)
    low = (table - high.astype(np.float64)).astype(ml_dtypes.bfloat16)
    return np.stack([high, low])


@functools.lru_cache(maxsize=None)
def tables():
    k = np.arange(FREQS)[:, None]
    p = np.arange(BLOCKS)[None, :]
    angle = 2.0 * np.pi * (k * p % OUTER) / OUTER
    outer = np.stack([np.cos(angle), -np.sin(angle)], axis=1)
    spread = np.einsum("kcp,rq->kcrpq", outer, np.eye(ROWS))
    spread = spread.reshape(FREQS * 2 * ROWS, BLOCKS * ROWS)
    b = np.arange(SPAN)
    angle = 2.0 * np.pi * (b[:, None] * b[None, :] % SPAN) / SPAN
    cos, sin = np.cos(angle), np.sin(angle)
    forward = np.block([[cos, -sin], [sin, cos]])
    backward = np.block([[cos, sin], [-sin, cos]])
    angle = 2.0 * np.pi * np.arange(PAD_FREQS)[:, None] * b[None, :] / TOTAL
    twist = np.stack([np.cos(angle), np.sin(angle)], axis=1)
    twist = np.broadcast_to(twist[:, :, None, :], (PAD_FREQS, 2, 8, SPAN))
    return (
        split16(spread),
        split16(forward),
        split16(backward),
        np.ascontiguousarray(twist.astype(np.float32)),
    )


def halves(x):
    high = x.astype(BF16)
    return high, (x - high.astype(F32)).astype(BF16)


def dot(a, b):
    return jnp.dot(a, b, preferred_element_type=F32)


def gate_kernel(k_ref, v_ref, q_ref, g_ref, out_ref):
    chans = k_ref.shape[1]
    first = k_ref[0].astype(F32) * v_ref[0].astype(F32)
    second = q_ref[0].astype(F32) * g_ref[0].astype(F32)
    shape = (chans // CHANS, CHANS, SPAN)
    both = jnp.concatenate([first.reshape(shape), second.reshape(shape)], axis=1)
    out_ref[...] = both.astype(BF16)


def gate(q_gate, k_gate, values, out_grad):
    chans = q_gate.shape[1]
    tile = min(chans, 1024)
    spec = pl.BlockSpec((1, tile, SPAN), lambda i: (0, i, 0))
    return pl.pallas_call(
        gate_kernel,
        grid=(chans // tile,),
        in_specs=[spec] * 4,
        out_specs=pl.BlockSpec((tile // CHANS, ROWS, SPAN), lambda i: (i, 0, 0)),
        out_shape=jax.ShapeDtypeStruct((chans // CHANS, ROWS, SPAN), BF16),
        name="gate",
    )(k_gate, values, q_gate, out_grad)


def correlate_kernel(x_ref, outer_ref, fwd_ref, bwd_ref, twist_ref, out_ref, high_ref, low_ref):
    seqs = x_ref.shape[0]
    cos = twist_ref[:, 0]
    sin = twist_ref[:, 1]

    def outer_step(s, carry):
        x = x_ref[pl.ds(2 * s, 2)].reshape(2, BLOCKS * ROWS, SPAN)
        x = jnp.concatenate([x[0], x[1]], axis=1)
        y2 = dot(outer_ref[0], x) + dot(outer_ref[1], x)
        c = cos[:FREQS, None]
        d = sin[:FREQS, None]
        for h in range(2):
            y = y2[:, h * SPAN : (h + 1) * SPAN].reshape(FREQS, 2, 2, CHANS, SPAN)
            real, imag = y[:, 0], y[:, 1]
            turned_real = (real * c + imag * d).reshape(FREQS, ROWS, SPAN)
            turned_imag = (imag * c - real * d).reshape(FREQS, ROWS, SPAN)
            rows = pl.ds(pl.multiple_of((2 * s + h) * ROWS, ROWS), ROWS)
            high, low = halves(turned_real)
            high_ref[:, rows, :SPAN] = high
            low_ref[:, rows, :SPAN] = low
            high, low = halves(turned_imag)
            high_ref[:, rows, SPAN:] = high
            low_ref[:, rows, SPAN:] = low
        return carry

    lax.fori_loop(0, seqs // 2, outer_step, 0, unroll=True)

    cross = []
    for k in range(FREQS):
        high = high_ref[k]
        spec = dot(high, fwd_ref[0]) + (dot(low_ref[k], fwd_ref[0]) + dot(high, fwd_ref[1]))
        spec = spec.reshape(seqs, 2, CHANS, 2 * SPAN)
        in_real, in_imag = spec[:, 0, :, :SPAN], spec[:, 0, :, SPAN:]
        grad_real, grad_imag = spec[:, 1, :, :SPAN], spec[:, 1, :, SPAN:]
        real = jnp.sum(in_real * grad_real + in_imag * grad_imag, axis=0)
        imag = jnp.sum(in_real * grad_imag - in_imag * grad_real, axis=0)
        cross.append(jnp.concatenate([real, imag], axis=1))
    cross.append(jnp.zeros((CHANS, 2 * SPAN), F32))
    cross = jnp.concatenate(cross, axis=0)

    high, low = halves(cross)
    back = dot(high, bwd_ref[0]) + (dot(low, bwd_ref[0]) + dot(high, bwd_ref[1]))
    back = back.reshape(PAD_FREQS, CHANS, 2 * SPAN)
    real, imag = back[:, :, :SPAN], back[:, :, SPAN:]
    turned_real = real * cos - imag * sin
    turned_imag = real * sin + imag * cos
    for n in range(BLOCKS):
        total = None
        for k in range(FREQS):
            weight = (1.0 if k in (0, BLOCKS) else 2.0) / TOTAL
            angle = 2.0 * math.pi * (k * n % OUTER) / OUTER
            term = turned_real[k] * (weight * math.cos(angle))
            if k * n % BLOCKS:
                term = term - turned_imag[k] * (weight * math.sin(angle))
            total = term if total is None else total + term
        out_ref[n] = total.astype(BF16)


def correlate(x):
    seqs = x.shape[0]
    outer, forward, backward, twist = tables()
    rows = seqs * ROWS
    flops = 2 * seqs * 2 * outer.shape[1] * outer.shape[2] * SPAN + 6 * FREQS * rows * 4 * SPAN * SPAN
    return pl.pallas_call(
        correlate_kernel,
        in_specs=[pl.BlockSpec(memory_space=pltpu.VMEM)] * 5,
        out_specs=pl.BlockSpec(memory_space=pltpu.VMEM),
        out_shape=jax.ShapeDtypeStruct((BLOCKS, CHANS, SPAN), BF16),
        scratch_shapes=[
            pltpu.VMEM((FREQS, rows, 2 * SPAN), BF16),
            pltpu.VMEM((FREQS, rows, 2 * SPAN), BF16),
        ],
        compiler_params=pltpu.CompilerParams(vmem_limit_bytes=32 * 1024 * 1024),
        cost_estimate=pl.CostEstimate(flops=flops, bytes_accessed=3_000_000, transcendentals=0),
        name="correlate",
    )(x, outer, forward, backward, twist)


CTX = ("x", "y_hi", "core")
NEAR = ("y_lo", "z_lo")


def to_each(x, axes):
    return lax.all_to_all(x, axes, split_axis=0, concat_axis=0, tiled=True)


def sum_far(part):
    far = lax.axis_size("z_hi")
    here = lax.axis_index("z_hi")
    held = [part]
    for step in range(1, far):
        held.append(lax.ppermute(part, "z_hi", [(i, (i + step) % far) for i in range(far)]))
    held = [x.astype(F32) for x in held]
    total = None
    for place in range(far):
        term = held[0]
        for step in range(1, far):
            term = jnp.where((here - place) % far == step, held[step], term)
        total = term if total is None else total + term
    return total


def body(length, batch, q_gate, k_gate, values, out_grad, decay):
    near = lax.axis_size(NEAR)
    gated = gate(q_gate, k_gate, values, out_grad)
    whole = to_each(gated, NEAR + CTX)
    part = correlate(whole.reshape(near, BLOCKS, ROWS, SPAN))

    first = (lax.axis_index(NEAR) * BLOCKS + lax.axis_index(CTX)) * CHANS
    mine = lax.dynamic_slice_in_dim(decay, first, CHANS)
    lags = jnp.arange(length, dtype=jnp.int32).astype(F32).reshape(BLOCKS, 1, SPAN)
    window = jnp.exp(-mine[None, :, None] * lags / length) / math.sqrt(batch * length)
    ours = (sum_far(part) * window).astype(BF16)

    sent = jnp.broadcast_to(ours[None], (near, BLOCKS, CHANS, SPAN))
    everyone = to_each(sent.reshape(near * BLOCKS, CHANS, SPAN), NEAR + CTX)
    return everyone.reshape(near * BLOCKS * CHANS, SPAN).astype(F32)


def solution(mesh):
    dp, ctx = mesh.devices.shape
    fine = Mesh(
        mesh.devices.reshape(4, dp // 16, 4, ctx // 4, 2, 2),
        ("y_lo", "z_hi", "z_lo") + CTX,
    )
    seqs = ("y_lo", "z_hi", "z_lo")
    return jax.shard_map(
        functools.partial(body, SPAN * ctx, dp),
        mesh=fine,
        in_specs=(P(seqs, None, CTX),) * 4 + (P(),),
        out_specs=P(None, CTX),
        check_vma=False,
    )
```

```python
import functools
import math

import jax
import jax.numpy as jnp
import ml_dtypes
import numpy as np
from jax import lax
from jax.experimental import pallas as pl
from jax.experimental.pallas import tpu as pltpu
from jax.sharding import Mesh, PartitionSpec as P

F32 = jnp.float32
BF16 = jnp.bfloat16

SPAN = 128
BLOCKS = 16
FREQS = BLOCKS + 1
PAD_FREQS = FREQS + 1
ROWS = 16
CHANS = ROWS // 2
OUTER = 2 * BLOCKS
TOTAL = OUTER * SPAN


def split16(table):
    high = table.astype(ml_dtypes.bfloat16)
    low = (table - high.astype(np.float64)).astype(ml_dtypes.bfloat16)
    return np.stack([high, low])


@functools.lru_cache(maxsize=None)
def tables():
    k = np.arange(FREQS)[:, None]
    p = np.arange(BLOCKS)[None, :]
    angle = 2.0 * np.pi * (k * p % OUTER) / OUTER
    outer = np.stack([np.cos(angle), -np.sin(angle)], axis=1)
    spread = np.einsum("kcp,rq->kcrpq", outer, np.eye(ROWS))
    spread = spread.reshape(FREQS * 2 * ROWS, BLOCKS * ROWS)
    b = np.arange(SPAN)
    angle = 2.0 * np.pi * (b[:, None] * b[None, :] % SPAN) / SPAN
    cos, sin = np.cos(angle), np.sin(angle)
    forward = np.block([[cos, -sin], [sin, cos]])
    backward = np.block([[cos, sin], [-sin, cos]])
    angle = 2.0 * np.pi * np.arange(PAD_FREQS)[:, None] * b[None, :] / TOTAL
    twist = np.stack([np.cos(angle), np.sin(angle)], axis=1)
    twist = np.broadcast_to(twist[:, :, None, :], (PAD_FREQS, 2, 8, SPAN))
    return (
        split16(spread),
        split16(forward),
        split16(backward),
        np.ascontiguousarray(twist.astype(np.float32)),
    )


def halves(x):
    high = x.astype(BF16)
    return high, (x - high.astype(F32)).astype(BF16)


def dot(a, b):
    return jnp.dot(a, b, preferred_element_type=F32)


def gate_kernel(k_ref, v_ref, q_ref, g_ref, out_ref):
    chans = k_ref.shape[1]
    first = k_ref[0].astype(F32) * v_ref[0].astype(F32)
    second = q_ref[0].astype(F32) * g_ref[0].astype(F32)
    shape = (chans // CHANS, CHANS, SPAN)
    both = jnp.concatenate([first.reshape(shape), second.reshape(shape)], axis=1)
    out_ref[...] = both.astype(BF16)


def gate(q_gate, k_gate, values, out_grad):
    chans = q_gate.shape[1]
    tile = min(chans, 1024)
    spec = pl.BlockSpec((1, tile, SPAN), lambda i: (0, i, 0))
    return pl.pallas_call(
        gate_kernel,
        grid=(chans // tile,),
        in_specs=[spec] * 4,
        out_specs=pl.BlockSpec((tile // CHANS, ROWS, SPAN), lambda i: (i, 0, 0)),
        out_shape=jax.ShapeDtypeStruct((chans // CHANS, ROWS, SPAN), BF16),
        name="gate",
    )(k_gate, values, q_gate, out_grad)


def correlate_kernel(x_ref, outer_ref, fwd_ref, bwd_ref, twist_ref, out_ref, high_ref, low_ref):
    seqs = x_ref.shape[0]
    cos = twist_ref[:, 0]
    sin = twist_ref[:, 1]

    def outer_step(s, carry):
        x = x_ref[pl.ds(2 * s, 2)].reshape(2, BLOCKS * ROWS, SPAN)
        x = jnp.concatenate([x[0], x[1]], axis=1)
        y2 = dot(outer_ref[0], x) + dot(outer_ref[1], x)
        c = cos[:FREQS, None]
        d = sin[:FREQS, None]
        for h in range(2):
            y = y2[:, h * SPAN : (h + 1) * SPAN].reshape(FREQS, 2, 2, CHANS, SPAN)
            real, imag = y[:, 0], y[:, 1]
            turned_real = (real * c + imag * d).reshape(FREQS, ROWS, SPAN)
            turned_imag = (imag * c - real * d).reshape(FREQS, ROWS, SPAN)
            rows = pl.ds(pl.multiple_of((2 * s + h) * ROWS, ROWS), ROWS)
            high, low = halves(turned_real)
            high_ref[:, rows, :SPAN] = high
            low_ref[:, rows, :SPAN] = low
            high, low = halves(turned_imag)
            high_ref[:, rows, SPAN:] = high
            low_ref[:, rows, SPAN:] = low
        return carry

    lax.fori_loop(0, seqs // 2, outer_step, 0, unroll=True)

    cross = []
    for k in range(FREQS):
        high = high_ref[k]
        spec = dot(high, fwd_ref[0]) + (dot(low_ref[k], fwd_ref[0]) + dot(high, fwd_ref[1]))
        spec = spec.reshape(seqs, 2, CHANS, 2 * SPAN)
        in_real, in_imag = spec[:, 0, :, :SPAN], spec[:, 0, :, SPAN:]
        grad_real, grad_imag = spec[:, 1, :, :SPAN], spec[:, 1, :, SPAN:]
        real = jnp.sum(in_real * grad_real + in_imag * grad_imag, axis=0)
        imag = jnp.sum(in_real * grad_imag - in_imag * grad_real, axis=0)
        cross.append(jnp.concatenate([real, imag], axis=1))
    cross.append(jnp.zeros((CHANS, 2 * SPAN), F32))
    cross = jnp.concatenate(cross, axis=0)

    high, low = halves(cross)
    back = dot(high, bwd_ref[0]) + (dot(low, bwd_ref[0]) + dot(high, bwd_ref[1]))
    back = back.reshape(PAD_FREQS, CHANS, 2 * SPAN)
    real, imag = back[:, :, :SPAN], back[:, :, SPAN:]
    turned_real = real * cos - imag * sin
    turned_imag = real * sin + imag * cos
    for n in range(BLOCKS):
        total = None
        for k in range(FREQS):
            weight = (1.0 if k in (0, BLOCKS) else 2.0) / TOTAL
            angle = 2.0 * math.pi * (k * n % OUTER) / OUTER
            term = turned_real[k] * (weight * math.cos(angle))
            if k * n % BLOCKS:
                term = term - turned_imag[k] * (weight * math.sin(angle))
            total = term if total is None else total + term
        out_ref[n] = total.astype(BF16)


def correlate(x):
    seqs = x.shape[0]
    outer, forward, backward, twist = tables()
    rows = seqs * ROWS
    flops = 2 * seqs * 2 * outer.shape[1] * outer.shape[2] * SPAN + 6 * FREQS * rows * 4 * SPAN * SPAN
    return pl.pallas_call(
        correlate_kernel,
        in_specs=[pl.BlockSpec(memory_space=pltpu.VMEM)] * 5,
        out_specs=pl.BlockSpec(memory_space=pltpu.VMEM),
        out_shape=jax.ShapeDtypeStruct((BLOCKS, CHANS, SPAN), BF16),
        scratch_shapes=[
            pltpu.VMEM((FREQS, rows, 2 * SPAN), BF16),
            pltpu.VMEM((FREQS, rows, 2 * SPAN), BF16),
        ],
        compiler_params=pltpu.CompilerParams(vmem_limit_bytes=32 * 1024 * 1024),
        cost_estimate=pl.CostEstimate(flops=flops, bytes_accessed=3_000_000, transcendentals=0),
        name="correlate",
    )(x, outer, forward, backward, twist)


CTX = ("x", "y_hi", "core")
NEAR = ("y_lo", "z_lo")


def to_each(x, axes):
    return lax.all_to_all(x, axes, split_axis=0, concat_axis=0, tiled=True)


def body(length, batch, q_gate, k_gate, values, out_grad, decay):
    near = lax.axis_size(NEAR)
    gated = gate(q_gate, k_gate, values, out_grad)
    whole = to_each(gated, NEAR + CTX)
    part = correlate(whole.reshape(near, BLOCKS, ROWS, SPAN))

    first = (lax.axis_index(NEAR) * BLOCKS + lax.axis_index(CTX)) * CHANS
    mine = lax.dynamic_slice_in_dim(decay, first, CHANS)
    lags = jnp.arange(length, dtype=jnp.int32).astype(F32).reshape(BLOCKS, 1, SPAN)
    window = jnp.exp(-mine[None, :, None] * lags / length) / math.sqrt(batch * length)
    parts = lax.all_gather(part, "z_hi", axis=0)
    ours = (jnp.sum(parts.astype(F32), axis=0) * window).astype(BF16)

    sent = jnp.broadcast_to(ours[None], (near, BLOCKS, CHANS, SPAN))
    everyone = to_each(sent.reshape(near * BLOCKS, CHANS, SPAN), NEAR + CTX)
    return everyone.reshape(near * BLOCKS * CHANS, SPAN).astype(F32)


def solution(mesh):
    dp, ctx = mesh.devices.shape
    fine = Mesh(
        mesh.devices.reshape(4, dp // 16, 4, ctx // 4, 2, 2),
        ("y_lo", "z_hi", "z_lo") + CTX,
    )
    seqs = ("y_lo", "z_hi", "z_lo")
    return jax.shard_map(
        functools.partial(body, SPAN * ctx, dp),
        mesh=fine,
        in_specs=(P(seqs, None, CTX),) * 4 + (P(),),
        out_specs=P(None, CTX),
        check_vma=False,
    )
```

```python
import functools
import math

import jax
import jax.numpy as jnp
import ml_dtypes
import numpy as np
from jax import lax
from jax.experimental import pallas as pl
from jax.experimental.pallas import tpu as pltpu
from jax.sharding import Mesh, PartitionSpec as P

F32 = jnp.float32
BF16 = jnp.bfloat16

SPAN = 128
BLOCKS = 16
FREQS = BLOCKS + 1
PAD_FREQS = FREQS + 1
ROWS = 16
CHANS = ROWS // 2
OUTER = 2 * BLOCKS
TOTAL = OUTER * SPAN


def split16(table):
    high = table.astype(ml_dtypes.bfloat16)
    low = (table - high.astype(np.float64)).astype(ml_dtypes.bfloat16)
    return np.stack([high, low])


@functools.lru_cache(maxsize=None)
def tables():
    k = np.arange(FREQS)[:, None]
    p = np.arange(BLOCKS)[None, :]
    angle = 2.0 * np.pi * (k * p % OUTER) / OUTER
    outer = np.stack([np.cos(angle), -np.sin(angle)], axis=1)
    spread = np.einsum("kcp,rq->kcrpq", outer, np.eye(ROWS))
    spread = spread.reshape(FREQS * 2 * ROWS, BLOCKS * ROWS)
    b = np.arange(SPAN)
    angle = 2.0 * np.pi * (b[:, None] * b[None, :] % SPAN) / SPAN
    cos, sin = np.cos(angle), np.sin(angle)
    forward = np.block([[cos, -sin], [sin, cos]])
    backward = np.block([[cos, sin], [-sin, cos]])
    angle = 2.0 * np.pi * np.arange(PAD_FREQS)[:, None] * b[None, :] / TOTAL
    twist = np.stack([np.cos(angle), np.sin(angle)], axis=1)
    twist = np.broadcast_to(twist[:, :, None, :], (PAD_FREQS, 2, 8, SPAN))
    return (
        split16(spread),
        split16(forward),
        split16(backward),
        np.ascontiguousarray(twist.astype(np.float32)),
    )


def halves(x):
    high = x.astype(BF16)
    return high, (x - high.astype(F32)).astype(BF16)


def dot(a, b):
    return jnp.dot(a, b, preferred_element_type=F32)


def gate_kernel(k_ref, v_ref, q_ref, g_ref, out_ref):
    chans = k_ref.shape[1]
    first = k_ref[0].astype(F32) * v_ref[0].astype(F32)
    second = q_ref[0].astype(F32) * g_ref[0].astype(F32)
    shape = (chans // CHANS, CHANS, SPAN)
    both = jnp.concatenate([first.reshape(shape), second.reshape(shape)], axis=1)
    out_ref[...] = both.astype(BF16)


def gate(q_gate, k_gate, values, out_grad):
    chans = q_gate.shape[1]
    tile = min(chans, 1024)
    spec = pl.BlockSpec((1, tile, SPAN), lambda i: (0, i, 0))
    return pl.pallas_call(
        gate_kernel,
        grid=(chans // tile,),
        in_specs=[spec] * 4,
        out_specs=pl.BlockSpec((tile // CHANS, ROWS, SPAN), lambda i: (i, 0, 0)),
        out_shape=jax.ShapeDtypeStruct((chans // CHANS, ROWS, SPAN), BF16),
        name="gate",
    )(k_gate, values, q_gate, out_grad)


def correlate_kernel(x_ref, outer_ref, fwd_ref, bwd_ref, twist_ref, out_ref, high_ref, low_ref):
    seqs = x_ref.shape[0]
    copies = out_ref.shape[0]
    cos = twist_ref[:, 0]
    sin = twist_ref[:, 1]

    def outer_step(s, carry):
        x = x_ref[pl.ds(2 * s, 2)].reshape(2, BLOCKS * ROWS, SPAN)
        x = jnp.concatenate([x[0], x[1]], axis=1)
        y2 = dot(outer_ref[0], x) + dot(outer_ref[1], x)
        c = cos[:FREQS, None]
        d = sin[:FREQS, None]
        for h in range(2):
            y = y2[:, h * SPAN : (h + 1) * SPAN].reshape(FREQS, 2, 2, CHANS, SPAN)
            real, imag = y[:, 0], y[:, 1]
            turned_real = (real * c + imag * d).reshape(FREQS, ROWS, SPAN)
            turned_imag = (imag * c - real * d).reshape(FREQS, ROWS, SPAN)
            rows = pl.ds(pl.multiple_of((2 * s + h) * ROWS, ROWS), ROWS)
            high, low = halves(turned_real)
            high_ref[:, rows, :SPAN] = high
            low_ref[:, rows, :SPAN] = low
            high, low = halves(turned_imag)
            high_ref[:, rows, SPAN:] = high
            low_ref[:, rows, SPAN:] = low
        return carry

    lax.fori_loop(0, seqs // 2, outer_step, 0, unroll=True)

    cross = []
    for k in range(FREQS):
        high = high_ref[k]
        spec = dot(high, fwd_ref[0]) + (dot(low_ref[k], fwd_ref[0]) + dot(high, fwd_ref[1]))
        spec = spec.reshape(seqs, 2, CHANS, 2 * SPAN)
        in_real, in_imag = spec[:, 0, :, :SPAN], spec[:, 0, :, SPAN:]
        grad_real, grad_imag = spec[:, 1, :, :SPAN], spec[:, 1, :, SPAN:]
        real = jnp.sum(in_real * grad_real + in_imag * grad_imag, axis=0)
        imag = jnp.sum(in_real * grad_imag - in_imag * grad_real, axis=0)
        cross.append(jnp.concatenate([real, imag], axis=1))
    cross.append(jnp.zeros((CHANS, 2 * SPAN), F32))
    cross = jnp.concatenate(cross, axis=0)

    high, low = halves(cross)
    back = dot(high, bwd_ref[0]) + (dot(low, bwd_ref[0]) + dot(high, bwd_ref[1]))
    back = back.reshape(PAD_FREQS, CHANS, 2 * SPAN)
    real, imag = back[:, :, :SPAN], back[:, :, SPAN:]
    turned_real = real * cos - imag * sin
    turned_imag = real * sin + imag * cos
    for n in range(BLOCKS):
        total = None
        for k in range(FREQS):
            weight = (1.0 if k in (0, BLOCKS) else 2.0) / TOTAL
            angle = 2.0 * math.pi * (k * n % OUTER) / OUTER
            term = turned_real[k] * (weight * math.cos(angle))
            if k * n % BLOCKS:
                term = term - turned_imag[k] * (weight * math.sin(angle))
            total = term if total is None else total + term
        for copy in range(copies):
            out_ref[copy, n] = total.astype(BF16)


def correlate(x, copies):
    seqs = x.shape[0]
    outer, forward, backward, twist = tables()
    rows = seqs * ROWS
    flops = 2 * seqs * 2 * outer.shape[1] * outer.shape[2] * SPAN + 6 * FREQS * rows * 4 * SPAN * SPAN
    return pl.pallas_call(
        correlate_kernel,
        in_specs=[pl.BlockSpec(memory_space=pltpu.VMEM)] * 5,
        out_specs=pl.BlockSpec(memory_space=pltpu.VMEM),
        out_shape=jax.ShapeDtypeStruct((copies, BLOCKS, CHANS, SPAN), BF16),
        scratch_shapes=[
            pltpu.VMEM((FREQS, rows, 2 * SPAN), BF16),
            pltpu.VMEM((FREQS, rows, 2 * SPAN), BF16),
        ],
        compiler_params=pltpu.CompilerParams(vmem_limit_bytes=32 * 1024 * 1024),
        cost_estimate=pl.CostEstimate(flops=flops, bytes_accessed=3_000_000, transcendentals=0),
        name="correlate",
    )(x, outer, forward, backward, twist)


CTX = ("x", "y_hi", "core")
NEAR = ("y_lo", "z_lo")


def to_each(x, axes):
    return lax.all_to_all(x, axes, split_axis=0, concat_axis=0, tiled=True)


def body(length, batch, q_gate, k_gate, values, out_grad, decay):
    near = lax.axis_size(NEAR)
    gated = gate(q_gate, k_gate, values, out_grad)
    whole = to_each(gated, NEAR + CTX)

    first = (lax.axis_index(NEAR) * BLOCKS + lax.axis_index(CTX)) * CHANS
    mine = lax.dynamic_slice_in_dim(decay, first, CHANS)
    lags = jnp.arange(length, dtype=jnp.int32).astype(F32).reshape(BLOCKS, 1, SPAN)
    window = jnp.exp(-mine[None, :, None] * lags / length) / math.sqrt(batch * length)
    whole, window = lax.optimization_barrier((whole, window))

    part = correlate(whole.reshape(near, BLOCKS, ROWS, SPAN), lax.axis_size("z_hi"))
    parts = to_each(part, "z_hi")
    ours = (jnp.sum(parts.astype(F32), axis=0) * window).astype(BF16)

    sent = jnp.broadcast_to(ours[None], (near, BLOCKS, CHANS, SPAN))
    everyone = to_each(sent.reshape(near * BLOCKS, CHANS, SPAN), NEAR + CTX)
    return everyone.reshape(near * BLOCKS * CHANS, SPAN).astype(F32)


def solution(mesh):
    dp, ctx = mesh.devices.shape
    fine = Mesh(
        mesh.devices.reshape(4, dp // 16, 4, ctx // 4, 2, 2),
        ("y_lo", "z_hi", "z_lo") + CTX,
    )
    seqs = ("y_lo", "z_hi", "z_lo")
    return jax.shard_map(
        functools.partial(body, SPAN * ctx, dp),
        mesh=fine,
        in_specs=(P(seqs, None, CTX),) * 4 + (P(),),
        out_specs=P(None, CTX),
        check_vma=False,
    )
```

```python
import functools
import math

import jax
import jax.numpy as jnp
import ml_dtypes
import numpy as np
from jax import lax
from jax.experimental import pallas as pl
from jax.experimental.pallas import tpu as pltpu
from jax.sharding import Mesh, PartitionSpec as P

F32 = jnp.float32
BF16 = jnp.bfloat16

SPAN = 128
BLOCKS = 16
FREQS = BLOCKS + 1
PAD_FREQS = FREQS + 1
ROWS = 16
CHANS = ROWS // 2
OUTER = 2 * BLOCKS
TOTAL = OUTER * SPAN


def split16(table):
    high = table.astype(ml_dtypes.bfloat16)
    low = (table - high.astype(np.float64)).astype(ml_dtypes.bfloat16)
    return np.stack([high, low])


@functools.lru_cache(maxsize=None)
def tables():
    k = np.arange(FREQS)[:, None]
    p = np.arange(BLOCKS)[None, :]
    angle = 2.0 * np.pi * (k * p % OUTER) / OUTER
    outer = np.stack([np.cos(angle), -np.sin(angle)], axis=1)
    spread = np.einsum("kcp,rq->kcrpq", outer, np.eye(ROWS))
    spread = spread.reshape(FREQS * 2 * ROWS, BLOCKS * ROWS)
    b = np.arange(SPAN)
    angle = 2.0 * np.pi * (b[:, None] * b[None, :] % SPAN) / SPAN
    cos, sin = np.cos(angle), np.sin(angle)
    forward = np.block([[cos, -sin], [sin, cos]])
    backward = np.block([[cos, sin], [-sin, cos]])
    angle = 2.0 * np.pi * np.arange(PAD_FREQS)[:, None] * b[None, :] / TOTAL
    twist = np.stack([np.cos(angle), np.sin(angle)], axis=1)
    twist = np.broadcast_to(twist[:, :, None, :], (PAD_FREQS, 2, 8, SPAN))
    return (
        split16(spread),
        split16(forward),
        split16(backward),
        np.ascontiguousarray(twist.astype(np.float32)),
    )


def halves(x):
    high = x.astype(BF16)
    return high, (x - high.astype(F32)).astype(BF16)


def dot(a, b):
    return jnp.dot(a, b, preferred_element_type=F32)


def gate_kernel(k_ref, v_ref, q_ref, g_ref, out_ref):
    chans = k_ref.shape[1]
    first = k_ref[0].astype(F32) * v_ref[0].astype(F32)
    second = q_ref[0].astype(F32) * g_ref[0].astype(F32)
    shape = (chans // CHANS, CHANS, SPAN)
    both = jnp.concatenate([first.reshape(shape), second.reshape(shape)], axis=1)
    out_ref[...] = both.astype(BF16)


def gate(q_gate, k_gate, values, out_grad):
    chans = q_gate.shape[1]
    tile = min(chans, 1024)
    spec = pl.BlockSpec((1, tile, SPAN), lambda i: (0, i, 0))
    return pl.pallas_call(
        gate_kernel,
        grid=(chans // tile,),
        in_specs=[spec] * 4,
        out_specs=pl.BlockSpec((tile // CHANS, ROWS, SPAN), lambda i: (i, 0, 0)),
        out_shape=jax.ShapeDtypeStruct((chans // CHANS, ROWS, SPAN), BF16),
        name="gate",
    )(k_gate, values, q_gate, out_grad)


def correlate_kernel(x_ref, outer_ref, fwd_ref, bwd_ref, twist_ref, out_ref, high_ref, low_ref):
    seqs = x_ref.shape[0]
    copies = out_ref.shape[0]
    cos = twist_ref[:, 0]
    sin = twist_ref[:, 1]

    def outer_step(s, carry):
        x = x_ref[pl.ds(2 * s, 2)].reshape(2, BLOCKS * ROWS, SPAN)
        x = jnp.concatenate([x[0], x[1]], axis=1)
        y2 = dot(outer_ref[0], x) + dot(outer_ref[1], x)
        c = cos[:FREQS, None]
        d = sin[:FREQS, None]
        for h in range(2):
            y = y2[:, h * SPAN : (h + 1) * SPAN].reshape(FREQS, 2, 2, CHANS, SPAN)
            real, imag = y[:, 0], y[:, 1]
            turned_real = (real * c + imag * d).reshape(FREQS, ROWS, SPAN)
            turned_imag = (imag * c - real * d).reshape(FREQS, ROWS, SPAN)
            rows = pl.ds(pl.multiple_of((2 * s + h) * ROWS, ROWS), ROWS)
            high, low = halves(turned_real)
            high_ref[:, rows, :SPAN] = high
            low_ref[:, rows, :SPAN] = low
            high, low = halves(turned_imag)
            high_ref[:, rows, SPAN:] = high
            low_ref[:, rows, SPAN:] = low
        return carry

    lax.fori_loop(0, seqs // 2, outer_step, 0, unroll=True)

    cross = []
    for k in range(FREQS):
        high = high_ref[k]
        spec = dot(high, fwd_ref[0]) + (dot(low_ref[k], fwd_ref[0]) + dot(high, fwd_ref[1]))
        spec = spec.reshape(seqs, 2, CHANS, 2 * SPAN)
        in_real, in_imag = spec[:, 0, :, :SPAN], spec[:, 0, :, SPAN:]
        grad_real, grad_imag = spec[:, 1, :, :SPAN], spec[:, 1, :, SPAN:]
        real = jnp.sum(in_real * grad_real + in_imag * grad_imag, axis=0)
        imag = jnp.sum(in_real * grad_imag - in_imag * grad_real, axis=0)
        cross.append(jnp.concatenate([real, imag], axis=1))
    cross.append(jnp.zeros((CHANS, 2 * SPAN), F32))
    cross = jnp.concatenate(cross, axis=0)

    high, low = halves(cross)
    back = dot(high, bwd_ref[0]) + (dot(low, bwd_ref[0]) + dot(high, bwd_ref[1]))
    back = back.reshape(PAD_FREQS, CHANS, 2 * SPAN)
    real, imag = back[:, :, :SPAN], back[:, :, SPAN:]
    turned_real = real * cos - imag * sin
    turned_imag = real * sin + imag * cos
    for n in range(BLOCKS):
        total = None
        for k in range(FREQS):
            weight = (1.0 if k in (0, BLOCKS) else 2.0) / TOTAL
            angle = 2.0 * math.pi * (k * n % OUTER) / OUTER
            term = turned_real[k] * (weight * math.cos(angle))
            if k * n % BLOCKS:
                term = term - turned_imag[k] * (weight * math.sin(angle))
            total = term if total is None else total + term
        for copy in range(copies):
            out_ref[copy, n] = total.astype(BF16)


def correlate(x, copies):
    seqs = x.shape[0]
    outer, forward, backward, twist = tables()
    rows = seqs * ROWS
    flops = 2 * seqs * 2 * outer.shape[1] * outer.shape[2] * SPAN + 6 * FREQS * rows * 4 * SPAN * SPAN
    return pl.pallas_call(
        correlate_kernel,
        in_specs=[pl.BlockSpec(memory_space=pltpu.VMEM)] * 5,
        out_specs=pl.BlockSpec(memory_space=pltpu.VMEM),
        out_shape=jax.ShapeDtypeStruct((copies, BLOCKS, CHANS, SPAN), BF16),
        scratch_shapes=[
            pltpu.VMEM((FREQS, rows, 2 * SPAN), BF16),
            pltpu.VMEM((FREQS, rows, 2 * SPAN), BF16),
        ],
        compiler_params=pltpu.CompilerParams(vmem_limit_bytes=32 * 1024 * 1024),
        cost_estimate=pl.CostEstimate(flops=flops, bytes_accessed=3_000_000, transcendentals=0),
        name="correlate",
    )(x, outer, forward, backward, twist)


def finish_kernel(parts_ref, window_ref, out_ref):
    total = parts_ref[0].astype(F32)
    for place in range(1, parts_ref.shape[0]):
        total = total + parts_ref[place].astype(F32)
    ours = (total * window_ref[...]).astype(BF16)
    for copy in range(out_ref.shape[0]):
        out_ref[copy] = ours


def finish(parts, window, copies):
    return pl.pallas_call(
        finish_kernel,
        in_specs=[pl.BlockSpec(memory_space=pltpu.VMEM)] * 2,
        out_specs=pl.BlockSpec(memory_space=pltpu.VMEM),
        out_shape=jax.ShapeDtypeStruct((copies,) + window.shape, BF16),
        compiler_params=pltpu.CompilerParams(vmem_limit_bytes=16 * 1024 * 1024),
        name="finish",
    )(parts, window)


CTX = ("x", "y_hi", "core")
NEAR = ("y_lo", "z_lo")


def to_each(x, axes):
    return lax.all_to_all(x, axes, split_axis=0, concat_axis=0, tiled=True)


def body(length, batch, q_gate, k_gate, values, out_grad, decay):
    near = lax.axis_size(NEAR)
    gated = gate(q_gate, k_gate, values, out_grad)
    whole = to_each(gated, NEAR + CTX)

    first = (lax.axis_index(NEAR) * BLOCKS + lax.axis_index(CTX)) * CHANS
    mine = lax.dynamic_slice_in_dim(decay, first, CHANS)
    lags = jnp.arange(length, dtype=jnp.int32).astype(F32).reshape(BLOCKS, 1, SPAN)
    window = jnp.exp(-mine[None, :, None] * lags / length) / math.sqrt(batch * length)
    whole, window = lax.optimization_barrier((whole, window))

    part = correlate(whole.reshape(near, BLOCKS, ROWS, SPAN), lax.axis_size("z_hi"))
    parts = to_each(part, "z_hi")
    sent = finish(parts, window, near)
    everyone = to_each(sent.reshape(near * BLOCKS, CHANS, SPAN), NEAR + CTX)
    return everyone.reshape(near * BLOCKS * CHANS, SPAN).astype(F32)


def solution(mesh):
    dp, ctx = mesh.devices.shape
    fine = Mesh(
        mesh.devices.reshape(4, dp // 16, 4, ctx // 4, 2, 2),
        ("y_lo", "z_hi", "z_lo") + CTX,
    )
    seqs = ("y_lo", "z_hi", "z_lo")
    return jax.shard_map(
        functools.partial(body, SPAN * ctx, dp),
        mesh=fine,
        in_specs=(P(seqs, None, CTX),) * 4 + (P(),),
        out_specs=P(None, CTX),
        check_vma=False,
    )
```
